32 devices in a mesh: parts: 2 (over y), lat: 4 (over z), lon: 2 (over x), rep: 2 (over core).
Axes of the slice: x: 2, y: 2, z: 4, core: 2. Of those that a mesh axis runs over, the one named last changes fastest.
Arguments:
- observations: bfloat16 [1024, 256], P(('parts', 'lat', 'lon'), 'rep'), parts along dimension 0, may hold values from -6 to 6
- send_counts: int32 [16, 8], P(('parts', 'lat', 'lon')), parts along dimension 0, may hold values from 0 to 8, as said below
- bucket_slots: int32 [16, 8, 8], P(('parts', 'lat', 'lon')), parts along dimension 0, may hold values from 0 to 1024, as said below
- latent: bfloat16 [64, 64, 768], P(('parts', 'lat'), 'lon'), parts along dimension 0, may hold values from -6 to 6
- norm_gain: float32 [768], replicated, may hold values from 0.25 to 1.75
- w_query: bfloat16 [768, 768], P(None, 'rep'), may hold values from -0.21875 to 0.21875
- w_key: bfloat16 [256, 768], P(None, 'rep'), may hold values from -0.375 to 0.375
- w_value: bfloat16 [256, 768], P(None, 'rep'), may hold values from -0.375 to 0.375
- null_kv: bfloat16 [2, 768], P(None, 'rep'), may hold values from -8 to 8
- rel_bias: float32 [12, 25], P('rep')
- w_out: bfloat16 [768, 768], P('rep'), may hold values from -0.21875 to 0.21875
- w_up: bfloat16 [3072, 768], P(('lat', 'rep')), may hold values from -0.21875 to 0.21875
- w_down: bfloat16 [3072, 768], P(('lat', 'rep')), may hold values from -0.109375 to 0.109375
Outputs:
- updated: bfloat16 [64, 64, 768], P(('parts', 'lat', 'rep'), 'lon'), parts along dimension 0
The draws below stay inside these ranges and needn't reach their ends.
There are 2 independent parts, one for each index of `parts`. The reference program is written for one: setup_inputs(seed, part) draws one part's arguments, and reference() takes and returns one part's arrays. A program takes and returns all parts, laid end to end along the dimension named above; an argument that names none is the same for every part. Nothing has to cross between parts.
Inputs may be any that keep to these rules, and one draw needn't show every extreme that they name: `send_counts`: for each source the counts sum to at most 64; every source s sends 8 rows to owner s and to owner (s + 1) mod 8, and none to some other owner. `bucket_slots`: for owner d and source s, entry k is a slot below 1024 exactly when k < send_counts[s, d], and 1024 otherwise; the slots below 1024 of one owner are all different. `observations`: every row has a nonzero channel in each of its halves along the channels.
All inputs are finite; a program needn't handle non-finite values.
Results may differ from the reference program's by a relative error of at most 0.0054.
Values may be sent and summed in bfloat16 or wider, within the bound.
A program may use at most 192 MiB of HBM per device.

```python
import math
import jax
import jax.numpy as jnp
from jax import lax

D = 768
HEADS = 12
HEAD = 64
FF = 3072
CHAN = 256
BUCKET = 4
REACH = 2
CAP = 8
CLAT = 8
CLON = 32
NLAT = 32
NLON = 64
OWNERS = 8
OBS_DEV = 64
OBS = 512
SLOTS_DEV = 1024
WINDOW = 25
N_LAT = 4
N_LON = 2


def routing_tables(key):
    owner_index = jnp.arange(OWNERS, dtype=jnp.int32)
    dense = jax.random.randint(jax.random.fold_in(key, 11), (OWNERS,), 0, 3) == 0
    heavy = jax.random.randint(jax.random.fold_in(key, 12), (OWNERS, OWNERS), CAP // 2, CAP + 1)
    light = jax.random.randint(jax.random.fold_in(key, 13), (OWNERS, OWNERS), 0, CAP // 2 + 1)
    counts = jnp.where(dense[None, :], heavy, light).astype(jnp.int32)
    empty_step = jax.random.randint(jax.random.fold_in(key, 15), (OWNERS,), 2, OWNERS).astype(jnp.int32)
    counts = counts.at[owner_index, (owner_index + empty_step) % OWNERS].set(0)
    counts = counts.at[owner_index, owner_index].set(CAP)
    counts = counts.at[owner_index, (owner_index + 1) % OWNERS].set(CAP)
    active = jnp.arange(CAP, dtype=jnp.int32)[None, None, :] < jnp.transpose(counts)[:, :, None]
    flat_active = active.reshape(OWNERS, OWNERS * CAP).astype(jnp.int32)
    rank = jnp.cumsum(flat_active, axis=1) - 1
    owner_keys = jax.random.split(jax.random.fold_in(key, 14), OWNERS)
    orders = jax.vmap(jax.random.permutation, in_axes=(0, None))(owner_keys, jnp.arange(SLOTS_DEV, dtype=jnp.int32))
    chosen = jnp.take_along_axis(orders, jnp.maximum(rank, 0), axis=1)
    slots = jnp.where(flat_active > 0, chosen, SLOTS_DEV).reshape(OWNERS, OWNERS, CAP).astype(jnp.int32)
    return (counts, slots)


def draw_send_counts(key, part):
    return routing_tables(key)[0]


def draw_bucket_slots(key, part):
    return routing_tables(key)[1]


def draw_rel_bias(key, part):
    key = jax.random.fold_in(key, 5)
    return jnp.clip(jax.random.normal(key, (HEADS, WINDOW), jnp.float32), -4.0, 4.0)


def level_of(key, shape, cuts, smallest, top_value):
    def one(axis_at, parts):
        steps = jax.random.uniform(jax.random.fold_in(jax.random.fold_in(key, 6), axis_at), (parts,), jnp.float32, smallest / len(cuts), top_value / len(cuts))
        return jnp.repeat(jnp.exp(steps), shape[axis_at] // parts).reshape((-1,) + (1,) * (len(shape) - axis_at - 1))

    factor_of = one(*cuts[0])
    for cut in cuts[1:]:
        factor_of = factor_of * one(*cut)
    return factor_of


def centred(own_key, dims, spread, reach, cuts=(), kind=jnp.bfloat16):
    values = jax.random.normal(own_key, dims, jnp.float32) * spread
    if len(cuts) > 0:
        values = level_of(own_key, dims, cuts, -0.22, 0.18) * values
    return jnp.clip(values, min=-reach, max=reach).astype(kind)


def setup_inputs(seed: int = 0, part: int = 0) -> dict:
    seeds = jax.random.split(jax.random.key(seed), 14)
    own_keys = jax.random.split(jax.random.fold_in(seeds[13], part), 14)
    observations = centred(own_keys[0], (OBS, CHAN), 1.0, 6.0, ((0, 8), (1, 2)))
    send_counts = draw_send_counts(jax.random.fold_in(jax.random.fold_in(seeds[13], part), 71), part)
    bucket_slots = draw_bucket_slots(jax.random.fold_in(jax.random.fold_in(seeds[13], part), 71), part)
    latent = centred(own_keys[3], (NLAT, NLON, D), 1.0, 6.0, ((0, 4), (1, 2)))
    norm_gain = jnp.clip(1.0 + 0.15 * jax.random.normal(seeds[4], (D,), jnp.float32), 0.25, 1.75)
    w_query = centred(seeds[5], (D, D), D ** -0.5, 0.21875, ((1, 2),))
    w_key = centred(seeds[6], (CHAN, D), CHAN ** -0.5, 0.375, ((1, 2),))
    w_value = centred(seeds[7], (CHAN, D), CHAN ** -0.5, 0.375, ((1, 2),))
    null_kv = centred(seeds[8], (2, D), 2.0, 8.0, ((1, 2),))
    rel_bias = draw_rel_bias(jax.random.fold_in(seeds[13], 71), part)
    w_out = centred(seeds[10], (D, D), D ** -0.5, 0.21875, ((0, 2),))
    w_up = centred(seeds[11], (FF, D), D ** -0.5, 0.21875, ((0, 8),))
    w_down = centred(seeds[12], (FF, D), FF ** -0.5, 0.109375, ((0, 8),))
    return {"observations": observations, "send_counts": send_counts, "bucket_slots": bucket_slots, "latent": latent, "norm_gain": norm_gain, "w_query": w_query, "w_key": w_key, "w_value": w_value, "null_kv": null_kv, "rel_bias": rel_bias, "w_out": w_out, "w_up": w_up, "w_down": w_down}


def reference(observations, send_counts, bucket_slots, latent, norm_gain, w_query, w_key, w_value, null_kv, rel_bias, w_out, w_up, w_down):
    offsets = jnp.cumsum(send_counts, axis=1) - send_counts
    within = jnp.arange(CAP, dtype=jnp.int32)
    active = within[None, None, :] < send_counts[:, :, None]
    row_index = jnp.arange(OWNERS, dtype=jnp.int32)[:, None, None] * OBS_DEV + offsets[:, :, None] + within[None, None, :]
    row_index = jnp.where(active, row_index, 0).astype(jnp.int32)
    sent = jnp.where(active[..., None], observations[row_index], jnp.zeros((), observations.dtype))
    by_owner = jnp.transpose(sent, (1, 0, 2, 3)).reshape(-1, CHAN)
    target = (jnp.arange(OWNERS, dtype=jnp.int32)[:, None, None] * (SLOTS_DEV + 1) + bucket_slots).reshape(-1).astype(jnp.int32)
    slots_all = jnp.zeros((OWNERS * (SLOTS_DEV + 1), CHAN), observations.dtype).at[target].set(by_owner)
    slots_all = slots_all.reshape(OWNERS, SLOTS_DEV + 1, CHAN)[:, :SLOTS_DEV]
    obs_grid = slots_all.reshape(N_LAT, N_LON, CLAT, CLON, BUCKET, CHAN)
    obs_grid = jnp.transpose(obs_grid, (0, 2, 1, 3, 4, 5)).reshape(NLAT, NLON, BUCKET, CHAN)
    filled = jnp.any(obs_grid != 0, axis=-1)
    keys = jnp.dot(obs_grid, w_key, preferred_element_type=jnp.float32).astype(jnp.bfloat16)
    values = jnp.dot(obs_grid, w_value, preferred_element_type=jnp.float32).astype(jnp.bfloat16)
    lat_float = latent.astype(jnp.float32)
    inv_rms = lax.rsqrt(lax.optimization_barrier(jnp.mean(lat_float * lat_float, axis=-1, keepdims=True)) + 1e-06)
    normed = (lat_float * inv_rms * norm_gain).astype(jnp.bfloat16)
    queries = jnp.dot(normed, w_query, preferred_element_type=jnp.float32).astype(jnp.bfloat16)

    def widen(grid):
        beside_all = jnp.concatenate([grid[:, -REACH:], grid, grid[:, :REACH]], axis=1)
        edge = jnp.zeros((REACH,) + beside_all.shape[1:], beside_all.dtype)
        return jnp.concatenate([edge, beside_all, edge], axis=0)
    keys_pad = widen(keys)
    values_pad = widen(values)
    filled_pad = widen(filled)
    window_side = 2 * REACH + 1
    score_scale = 1.0 / math.sqrt(HEAD)
    null_key = null_kv[0].astype(jnp.float32).reshape(HEADS, HEAD)
    null_value = null_kv[1].astype(jnp.float32).reshape(HEADS, HEAD)

    def row_update(row):
        key_band = lax.dynamic_slice_in_dim(keys_pad, row, window_side, 0)
        value_band = lax.dynamic_slice_in_dim(values_pad, row, window_side, 0)
        filled_band = lax.dynamic_slice_in_dim(filled_pad, row, window_side, 0)
        query_heads = lax.dynamic_index_in_dim(queries, row, 0, False).astype(jnp.float32).reshape(NLON, HEADS, HEAD)
        score_parts = [(jnp.einsum('xhe,he->xh', query_heads, null_key) * score_scale)[..., None]]
        for row_step in range(window_side):
            for col_step in range(window_side):
                window_keys = key_band[row_step, col_step:col_step + NLON].astype(jnp.float32).reshape(NLON, BUCKET, HEADS, HEAD)
                local_scores = jnp.einsum('xhe,xbhe->xhb', query_heads, window_keys) * score_scale
                local_scores = local_scores + rel_bias[:, row_step * window_side + col_step][None, :, None]
                window_mask = filled_band[row_step, col_step:col_step + NLON]
                score_parts.append(jnp.where(window_mask[:, None, :], local_scores, -jnp.inf))
        scores = jnp.concatenate(score_parts, axis=-1)
        row_max = lax.optimization_barrier(jnp.max(scores, axis=-1, keepdims=True))
        exponent = jnp.exp(scores - row_max)
        weights = (exponent / lax.optimization_barrier(jnp.sum(exponent, axis=-1, keepdims=True))).astype(jnp.bfloat16)
        mixture = weights[..., 0:1].astype(jnp.float32) * null_value[None]
        for row_step in range(window_side):
            for col_step in range(window_side):
                place = row_step * window_side + col_step
                window_values = value_band[row_step, col_step:col_step + NLON].astype(jnp.float32).reshape(NLON, BUCKET, HEADS, HEAD)
                share = weights[..., 1 + place * BUCKET:1 + (place + 1) * BUCKET].astype(jnp.float32)
                mixture = mixture + jnp.einsum('xhb,xbhe->xhe', share, window_values)
        mixture = mixture.astype(jnp.bfloat16).reshape(NLON, D)
        attended = jnp.dot(mixture, w_out, preferred_element_type=jnp.float32)
        normed_row = lax.dynamic_index_in_dim(normed, row, 0, False)
        raised = lax.dot_general(normed_row, w_up, (((1,), (1,)), ((), ())), preferred_element_type=jnp.float32)
        hidden = jax.nn.gelu(raised, approximate=True).astype(jnp.bfloat16)
        expanded = jnp.dot(hidden, w_down, preferred_element_type=jnp.float32)
        latent_row = lax.dynamic_index_in_dim(lat_float, row, 0, False)
        return (latent_row + attended + expanded).astype(jnp.bfloat16)
    return lax.map(row_update, jnp.arange(NLAT, dtype=jnp.int32))
```

```python
import functools
import math

import jax
import jax.numpy as jnp
import numpy as np
from jax import lax
from jax.experimental import pallas as pl
from jax.experimental.pallas import tpu as pltpu
from jax.sharding import PartitionSpec as P

HEAD = 64
BUCKET = 4
REACH = 2
SIDE = 2 * REACH + 1
FAR = -128.0
LOW = -1e30
MESH = pl.DeviceIdType.MESH


def extended(cells, sides, width):
    for axis, dim in sides:
        count = lax.axis_size(axis)
        head = lax.slice_in_dim(cells, 0, width, axis=dim)
        tail = lax.slice_in_dim(cells, cells.shape[dim] - width, cells.shape[dim], axis=dim)
        cells = jnp.concatenate(
            [
                lax.ppermute(tail, axis, [(i, (i + 1) % count) for i in range(count)]),
                cells,
                lax.ppermute(head, axis, [((i + 1) % count, i) for i in range(count)]),
            ],
            axis=dim,
        )
    return cells


def banded(
    observations,
    send_counts,
    bucket_slots,
    latent,
    norm_gain,
    w_query,
    w_key,
    w_value,
    null_kv,
    rel_bias,
    w_out,
    w_up,
    w_down,
):
    counts = send_counts[0]
    places = bucket_slots.shape[2]
    half_chan = observations.shape[1]
    offsets = jnp.cumsum(counts) - counts
    within = jnp.arange(places, dtype=jnp.int32)
    active = within[None, :] < counts[:, None]
    picked = jnp.where(active, offsets[:, None] + within[None, :], 0)
    packed = jnp.where(active[:, :, None], observations[picked], jnp.zeros((), jnp.bfloat16))
    arrived = lax.all_to_all(packed, ("lat", "lon"), split_axis=0, concat_axis=0, tiled=True)
    lat_cells = latent.shape[0]
    lon_cells = latent.shape[1]
    slot_total = lat_cells * lon_cells * BUCKET
    target = bucket_slots[0].reshape(-1)
    slot_rows = (
        jnp.zeros((slot_total + 1, half_chan), jnp.bfloat16)
        .at[target]
        .set(arrived.reshape(-1, half_chan))
    )
    buckets = slot_rows[:slot_total].reshape(lat_cells, lon_cells, BUCKET, half_chan)
    rows_ext = lax.axis_index("lat") * lat_cells + jnp.arange(
        -REACH, lat_cells + REACH, dtype=jnp.int32
    )
    inside = (rows_ext >= 0) & (rows_ext < lat_cells * lax.axis_size("lat"))
    padded = extended(buckets, (("lat", 0), ("lon", 1)), REACH)
    padded = jnp.where(inside[:, None, None, None], padded, jnp.zeros((), jnp.bfloat16))
    widened = lax.all_gather(padded, "rep", axis=3, tiled=True)
    keys_ext = jnp.dot(widened, w_key, preferred_element_type=jnp.float32).astype(jnp.bfloat16)
    values_ext = jnp.dot(widened, w_value, preferred_element_type=jnp.float32).astype(jnp.bfloat16)
    filled_ext = jnp.any(widened != 0, axis=-1)
    lat_float = latent.astype(jnp.float32)
    inv_rms = lax.rsqrt(jnp.mean(lat_float * lat_float, axis=-1, keepdims=True) + 1e-06)
    normed = (lat_float * inv_rms * norm_gain).astype(jnp.bfloat16)
    queries = jnp.dot(normed, w_query, preferred_element_type=jnp.float32).astype(jnp.bfloat16)
    heads_here = w_query.shape[1] // HEAD
    window_side = 2 * REACH + 1
    wide_cols = lon_cells + 2 * REACH
    query_heads = queries.reshape(lat_cells, lon_cells, heads_here, HEAD)
    key_heads = keys_ext.reshape(lat_cells + 2 * REACH, wide_cols, BUCKET, heads_here, HEAD)
    value_heads = values_ext.reshape(lat_cells + 2 * REACH, wide_cols, BUCKET, heads_here, HEAD)
    null_key = null_kv[0].reshape(heads_here, HEAD)
    null_value = null_kv[1].astype(jnp.float32).reshape(heads_here, HEAD)
    score_scale = 1.0 / math.sqrt(HEAD)
    null_scores = (
        jnp.einsum("yxhe,he->hyx", query_heads, null_key, preferred_element_type=jnp.float32)
        * score_scale
    )
    score_parts = [null_scores[..., None]]
    for row_step in range(window_side):
        for col_step in range(window_side):
            place = row_step * window_side + col_step
            window_keys = key_heads[
                row_step : row_step + lat_cells, col_step : col_step + lon_cells
            ]
            local_scores = (
                jnp.einsum(
                    "yxhe,yxbhe->hyxb", query_heads, window_keys, preferred_element_type=jnp.float32
                )
                * score_scale
            )
            local_scores = local_scores + rel_bias[:, place][:, None, None, None]
            window_mask = filled_ext[
                row_step : row_step + lat_cells, col_step : col_step + lon_cells
            ]
            score_parts.append(jnp.where(window_mask[None], local_scores, -jnp.inf))
    scores = jnp.concatenate(score_parts, axis=-1)
    row_max = jnp.max(scores, axis=-1, keepdims=True)
    exponent = jnp.exp(scores - row_max)
    weights = (exponent / jnp.sum(exponent, axis=-1, keepdims=True)).astype(jnp.bfloat16)
    null_share = jnp.transpose(weights[..., 0], (1, 2, 0)).astype(jnp.float32)
    mixture = null_share[..., None] * null_value[None, None]
    for row_step in range(window_side):
        for col_step in range(window_side):
            place = row_step * window_side + col_step
            window_values = value_heads[
                row_step : row_step + lat_cells, col_step : col_step + lon_cells
            ]
            share = weights[..., 1 + place * BUCKET : 1 + (place + 1) * BUCKET]
            mixture = mixture + jnp.einsum(
                "hyxb,yxbhe->yxhe", share, window_values, preferred_element_type=jnp.float32
            )
    mixed = mixture.astype(jnp.bfloat16).reshape(lat_cells * lon_cells, heads_here * HEAD)
    attended = jnp.dot(mixed, w_out, preferred_element_type=jnp.float32)
    flat_normed = normed.reshape(lat_cells * lon_cells, -1)
    raised = lax.dot_general(
        flat_normed,
        lax.all_gather(w_up, "lat", axis=0, tiled=True),
        (((1,), (1,)), ((), ())),
        preferred_element_type=jnp.float32,
    )
    hidden = jax.nn.gelu(raised, approximate=True).astype(jnp.bfloat16)
    down_rows = lax.all_gather(w_down, "lat", axis=0, tiled=True)
    expanded = jnp.dot(hidden, down_rows, preferred_element_type=jnp.float32)
    combined = (attended + expanded).reshape(lat_cells, lon_cells, -1)
    summed = lax.psum_scatter(combined, "rep", scatter_dimension=0, tiled=True)
    share_rows = summed.shape[0]
    own_rows = lax.dynamic_slice_in_dim(
        lat_float, lax.axis_index("rep") * share_rows, share_rows, 0
    )
    return (own_rows + summed).astype(jnp.bfloat16)


def flipped(index, step):
    bit = 1
    while bit <= step:
        if step & bit:
            index = index + bit - 2 * bit * ((index // bit) % 2)
        bit *= 2
    return index


def dot_nt(a, b):
    return lax.dot_general(a, b, (((1,), (1,)), ((), ())), preferred_element_type=jnp.float32)


def dot_nn(a, b):
    return jnp.dot(a, b, preferred_element_type=jnp.float32)


def fused_kernel(
    sizes,
    meta_ref,
    obs_ref,
    spread_ref,
    owner_ref,
    before_ref,
    equal_ref,
    place_ref,
    lat_ref,
    gain_ref,
    wq_ref,
    wk_ref,
    wv_ref,
    head_ref,
    wo_ref,
    up_ref,
    down_ref,
    out_ref,
    wq2_ref,
    wk2_ref,
    wv2_ref,
    head2_ref,
    wo2_ref,
    up2_ref,
    down2_ref,
    tok_ref,
    back_ref,
    part_ref,
    rows_ref,
    metas_ref,
    q_ref,
    k_ref,
    v_ref,
    near_ref,
    att_ref,
    pair_send,
    pair_recv,
    tok_send,
    tok_recv,
    part_send,
    part_recv,
    obs_send,
    obs_recv,
    meta_send,
    meta_recv,
):
    n_lat, n_lon, lat_cells, lon_cells, heads = sizes
    half_rows = lat_cells // 2
    tokens = half_rows * lon_cells
    owners = n_lat * n_lon
    group = owners * 2
    listed = obs_ref.shape[0]
    total = owners * listed
    lat = lax.axis_index("lat")
    lon = lax.axis_index("lon")
    rep = lax.axis_index("rep")
    owner = lat * n_lon + lon
    me = owner * 2 + rep

    def member(flat):
        return {"lat": flat // (2 * n_lon), "lon": (flat // 2) % n_lon, "rep": flat % 2}

    barrier = pltpu.get_barrier_semaphore()
    for step in range(1, group):
        pl.semaphore_signal(
            barrier, inc=1, device_id=member((me + step) % group), device_id_type=MESH
        )

    x = lat_ref[pl.ds(pl.multiple_of(rep * tokens, tokens), tokens), :].astype(jnp.float32)
    inv = lax.rsqrt(jnp.mean(x * x, axis=-1, keepdims=True) + 1e-06)
    normed = (x * inv * gain_ref[...]).astype(jnp.bfloat16)
    tok_ref[lat] = normed

    counts = meta_ref[2:3, :]
    first = jnp.sum(before_ref[...] * counts, axis=1, keepdims=True)
    held = jnp.sum(equal_ref[...] * counts, axis=1, keepdims=True)
    place = place_ref[...][:, 0:1]
    spots = lax.broadcasted_iota(jnp.int32, (listed, obs_ref.shape[0]), 1).astype(jnp.float32)
    pick = jnp.where((spots == first + place) & (place < held), 1.0, 0.0).astype(jnp.bfloat16)
    packed = dot_nn(pick, obs_ref[...]).astype(jnp.bfloat16)
    my_rows = pl.ds(pl.multiple_of(owner * listed, listed), listed)
    rows_ref[rep, my_rows, :] = packed
    metas_ref[owner] = meta_ref[...]

    pl.semaphore_wait(barrier, group - 1)

    def pair_copy(index, source, target):
        return pltpu.make_async_remote_copy(
            src_ref=source,
            dst_ref=target,
            send_sem=pair_send.at[index],
            recv_sem=pair_recv.at[index],
            device_id={"rep": 1 - rep},
            device_id_type=MESH,
        )

    up_copy = pair_copy(0, up_ref, up2_ref)
    down_copy = pair_copy(1, down_ref, down2_ref)
    wq_copy = pair_copy(2, wq_ref, wq2_ref)
    wk_copy = pair_copy(3, wk_ref, wk2_ref)
    wv_copy = pair_copy(4, wv_ref, wv2_ref)
    wo_copy = pair_copy(5, wo_ref, wo2_ref)
    head_copy = pair_copy(6, head_ref, head2_ref)

    tok_copies = []
    for step in range(1, n_lat):
        there = flipped(lat, step)
        copy = pltpu.make_async_remote_copy(
            src_ref=tok_ref.at[lat],
            dst_ref=tok_ref.at[lat],
            send_sem=tok_send.at[step],
            recv_sem=tok_recv.at[step],
            device_id={"lat": there},
            device_id_type=MESH,
        )
        tok_copies.append(copy)
        copy.start()
    for copy in (up_copy, down_copy, wq_copy, wk_copy, wv_copy, wo_copy, head_copy):
        copy.start()

    def obs_copy(step, flat):
        other = (me + step) % group
        source_rows = pl.ds(pl.multiple_of((flat // 2) * listed, listed), listed)
        return pltpu.make_async_remote_copy(
            src_ref=rows_ref.at[flat % 2, source_rows],
            dst_ref=rows_ref.at[flat % 2, source_rows],
            send_sem=obs_send.at[step],
            recv_sem=obs_recv.at[step],
            device_id=member(other),
            device_id_type=MESH,
        )

    def meta_copy(step, who):
        other = (owner + step) % owners
        return pltpu.make_async_remote_copy(
            src_ref=metas_ref.at[who],
            dst_ref=metas_ref.at[who],
            send_sem=meta_send.at[step],
            recv_sem=meta_recv.at[step],
            device_id={"lat": other // n_lon, "lon": other % n_lon},
            device_id_type=MESH,
        )

    for step in range(1, group):
        obs_copy(step, me).start()
    for step in range(1, owners):
        meta_copy(step, owner).start()

    halves = ((up_ref, down_ref), (up2_ref, down2_ref))

    def fed(value):
        result = None
        for up, down in halves:
            hidden = jax.nn.gelu(dot_nt(value, up[...]), approximate=True).astype(jnp.bfloat16)
            term = dot_nn(hidden, down[...])
            result = term if result is None else result + term
        return result

    up_copy.wait_recv()
    down_copy.wait_recv()
    part_copies = []
    for step in range(1, n_lat):
        there = flipped(lat, step)
        tok_copies[step - 1].wait_recv()
        back_ref[step] = fed(tok_ref[there]).astype(jnp.bfloat16)
        copy = pltpu.make_async_remote_copy(
            src_ref=back_ref.at[step],
            dst_ref=part_ref.at[step],
            send_sem=part_send.at[step],
            recv_sem=part_recv.at[step],
            device_id={"lat": there},
            device_id_type=MESH,
        )
        part_copies.append(copy)
        copy.start()

    att_ref[...] = x + fed(normed)

    for step in range(1, group):
        obs_copy(step, (me + group - step) % group).wait_recv()
    for step in range(1, owners):
        meta_copy(step, (owner + owners - step) % owners).wait_recv()

    spread = spread_ref[...]
    own_lane = owner_ref[...]
    y_all = metas_ref[:, 0, :].astype(jnp.bfloat16)
    x_all = metas_ref[:, 1, :].astype(jnp.bfloat16)
    key_y = jnp.sum(dot_nn(y_all, spread) * own_lane, axis=0, keepdims=True)
    key_x = jnp.sum(dot_nn(x_all, spread) * own_lane, axis=0, keepdims=True)
    query_x = (
        lax.broadcasted_iota(jnp.int32, (lon_cells, total), 0) + lon * lon_cells
    ).astype(jnp.float32)
    wide = float(n_lon * lon_cells)
    off_x = key_x - query_x + float(REACH)
    off_x = jnp.where(off_x < 0, off_x + wide, off_x)
    near_ref[...] = jnp.where(off_x >= wide, off_x - wide, off_x)
    query_y = (
        lax.broadcasted_iota(jnp.int32, (half_rows, total), 0)
        + (lat * lat_cells + rep * half_rows)
    ).astype(jnp.float32)
    off_y = key_y - query_y + float(REACH)

    widened = jnp.concatenate([rows_ref[0], rows_ref[1]], axis=1)
    wq_copy.wait_recv()
    wk_copy.wait_recv()
    wv_copy.wait_recv()
    wo_copy.wait_recv()
    head_copy.wait_recv()
    scale = 1.0 / math.sqrt(HEAD)

    for wq, wk, wv, wo, per_head in (
        (wq_ref, wk_ref, wv_ref, wo_ref, head_ref),
        (wq2_ref, wk2_ref, wv2_ref, wo2_ref, head2_ref),
    ):
        queries = (dot_nn(normed, wq[...]).astype(jnp.bfloat16) * scale).astype(jnp.bfloat16)
        keys = dot_nn(widened, wk[...]).astype(jnp.bfloat16)
        values = dot_nn(widened, wv[...]).astype(jnp.bfloat16)
        for h in range(heads):
            lanes = slice(h * HEAD, (h + 1) * HEAD)
            q_ref[h] = queries[:, lanes]
            k_ref[h] = keys[:, lanes]
            v_ref[h] = values[:, lanes]

        def one_head(h, carry):
            q = q_ref[h]
            info = per_head[h]
            null_key = info[0:1, :HEAD]
            null_value = info[1:2, :HEAD]
            scores = dot_nt(q, k_ref[h])
            null_score = jnp.sum(q.astype(jnp.float32) * null_key, axis=1, keepdims=True)
            shifts = []
            for q_step in range(SIDE):
                shift = jnp.full(off_y.shape, LOW, jnp.float32)
                for p_step in range(SIDE):
                    at = p_step * SIDE + q_step
                    shift = jnp.where(off_y == float(p_step), info[2:3, at : at + 1], shift)
                shifts.append(shift)
            near = near_ref[...]
            biases = []
            for row in range(half_rows):
                bias = jnp.full(near.shape, LOW, jnp.float32)
                for q_step in range(SIDE):
                    bias = jnp.where(
                        near == float(q_step), shifts[q_step][row : row + 1, :], bias
                    )
                biases.append(bias)
            scores = scores + jnp.concatenate(biases, axis=0)
            top = jnp.maximum(jnp.max(scores, axis=1, keepdims=True), null_score)
            grown = jnp.exp(scores - top)
            null_grown = jnp.exp(null_score - top)
            share = 1.0 / (jnp.sum(grown, axis=1, keepdims=True) + null_grown)
            weights = (grown * share).astype(jnp.bfloat16)
            null_weight = (null_grown * share).astype(jnp.bfloat16).astype(jnp.float32)
            mixed = (dot_nn(weights, v_ref[h]) + null_weight * null_value).astype(jnp.bfloat16)
            rows = pl.ds(pl.multiple_of(h * HEAD, HEAD), HEAD)
            att_ref[...] += dot_nn(mixed, wo[rows, :])
            return carry

        lax.fori_loop(0, heads, one_head, 0)

    result = att_ref[...]
    for step in range(1, n_lat):
        part_copies[step - 1].wait_recv()
        result = result + part_ref[step].astype(jnp.float32)
    out_ref[...] = result.astype(jnp.bfloat16)

    for copy in tok_copies + part_copies:
        copy.wait_send()
    for copy in (up_copy, down_copy, wq_copy, wk_copy, wv_copy, wo_copy, head_copy):
        copy.wait_send()
    for step in range(1, group):
        obs_copy(step, me).wait_send()
    for step in range(1, owners):
        meta_copy(step, owner).wait_send()


def fused(
    n_lat,
    n_lon,
    observations,
    send_counts,
    bucket_slots,
    latent,
    norm_gain,
    w_query,
    w_key,
    w_value,
    null_kv,
    rel_bias,
    w_out,
    w_up,
    w_down,
):
    lat_cells, lon_cells, depth = latent.shape
    owners = n_lat * n_lon
    cap = bucket_slots.shape[2]
    listed = observations.shape[0]
    total = owners * listed
    half_chan = observations.shape[1]
    heads = w_query.shape[1] // HEAD
    tokens = lat_cells * lon_cells // 2
    lanes = 128

    slots = bucket_slots[0].reshape(-1)
    row_slots = lon_cells * BUCKET
    valid = slots < lat_cells * row_slots
    cell_y = lax.axis_index("lat") * lat_cells + slots // row_slots
    cell_x = lax.axis_index("lon") * lon_cells + (slots // BUCKET) % lon_cells
    y_line = jnp.where(valid, cell_y.astype(jnp.float32), FAR)
    x_line = jnp.where(valid, cell_x.astype(jnp.float32), 0.0)
    count_line = send_counts[0].astype(jnp.float32)
    meta = jnp.zeros((8, lanes), jnp.float32)
    meta = jnp.concatenate(
        [
            jnp.pad(line, (0, lanes - line.shape[0]))[None]
            for line in (y_line, x_line, count_line)
        ]
        + [jnp.zeros((5, lanes), jnp.float32)],
        axis=0,
    )
    nulls = jnp.transpose(null_kv.astype(jnp.float32).reshape(2, heads, HEAD), (1, 0, 2))
    per_head = jnp.concatenate(
        [
            jnp.pad(nulls, ((0, 0), (0, 0), (0, lanes - HEAD))),
            jnp.pad(rel_bias, ((0, 0), (0, lanes - rel_bias.shape[1])))[:, None],
            jnp.zeros((heads, 5, lanes), jnp.float32),
        ],
        axis=1,
    )

    lane = np.arange(total)
    line = np.arange(lanes)
    entry = np.arange(listed)
    spread = line[:, None] == ((lane // (owners * cap)) * cap + lane % cap)[None]
    own_lane = np.arange(owners)[:, None] == ((lane // cap) % owners)[None]
    before = line[None] < (entry // cap)[:, None]
    equal = line[None] == (entry // cap)[:, None]
    places = np.broadcast_to((entry % cap)[:, None], (listed, lanes))

    bf16 = jnp.bfloat16
    args = (
        meta,
        observations,
        jnp.asarray(spread, bf16),
        jnp.asarray(own_lane, jnp.float32),
        jnp.asarray(before, jnp.float32),
        jnp.asarray(equal, jnp.float32),
        jnp.asarray(places, jnp.float32),
        latent.reshape(lat_cells * lon_cells, depth),
        norm_gain.reshape(1, depth),
        w_query,
        w_key,
        w_value,
        per_head,
        w_out,
        w_up,
        w_down,
    )
    dma = pltpu.SemaphoreType.DMA
    group = 2 * owners
    out = pl.pallas_call(
        functools.partial(fused_kernel, (n_lat, n_lon, lat_cells, lon_cells, heads)),
        out_shape=jax.ShapeDtypeStruct((tokens, depth), bf16),
        in_specs=[pl.BlockSpec(memory_space=pltpu.VMEM)] * len(args),
        out_specs=pl.BlockSpec(memory_space=pltpu.VMEM),
        scratch_shapes=[
            pltpu.VMEM(w_query.shape, bf16),
            pltpu.VMEM(w_key.shape, bf16),
            pltpu.VMEM(w_value.shape, bf16),
            pltpu.VMEM(per_head.shape, jnp.float32),
            pltpu.VMEM(w_out.shape, bf16),
            pltpu.VMEM(w_up.shape, bf16),
            pltpu.VMEM(w_down.shape, bf16),
            pltpu.VMEM((n_lat, tokens, depth), bf16),
            pltpu.VMEM((n_lat, tokens, depth), bf16),
            pltpu.VMEM((n_lat, tokens, depth), bf16),
            pltpu.VMEM((2, total, half_chan), bf16),
            pltpu.VMEM((owners,) + meta.shape, jnp.float32),
            pltpu.VMEM((heads, tokens, HEAD), bf16),
            pltpu.VMEM((heads, total, HEAD), bf16),
            pltpu.VMEM((heads, total, HEAD), bf16),
            pltpu.VMEM((lon_cells, total), jnp.float32),
            pltpu.VMEM((tokens, depth), jnp.float32),
            dma((7,)),
            dma((7,)),
            dma((n_lat,)),
            dma((n_lat,)),
            dma((n_lat,)),
            dma((n_lat,)),
            dma((group,)),
            dma((group,)),
            dma((owners,)),
            dma((owners,)),
        ],
        compiler_params=pltpu.CompilerParams(
            collective_id=0, has_side_effects=True, vmem_limit_bytes=48 * 2**20
        ),
    )(*args)
    return out.reshape(lat_cells // 2, lon_cells, depth)


def solution(mesh):
    in_specs = (
        P(("parts", "lat", "lon"), "rep"),
        P(("parts", "lat", "lon"), None),
        P(("parts", "lat", "lon"), None, None),
        P(("parts", "lat"), "lon", None),
        P(),
        P(None, "rep"),
        P(None, "rep"),
        P(None, "rep"),
        P(None, "rep"),
        P("rep", None),
        P("rep", None),
        P(("lat", "rep"), None),
        P(("lat", "rep"), None),
    )
    out_specs = P(("parts", "lat", "rep"), "lon", None)
    n_lat, n_lon, n_rep = mesh.shape["lat"], mesh.shape["lon"], mesh.shape["rep"]

    def local(observations, send_counts, bucket_slots, *rest):
        cap = bucket_slots.shape[2]
        listed = n_lat * n_lon * cap
        direct = (
            n_rep == 2
            and n_lat in (2, 4)
            and listed <= 128
            and observations.shape[0] == listed
        )
        step = functools.partial(fused, n_lat, n_lon) if direct else banded
        return step(observations, send_counts, bucket_slots, *rest)

    return jax.shard_map(local, mesh=mesh, in_specs=in_specs, out_specs=out_specs, check_vma=False)
```

```python
import functools
import math

import jax
import jax.numpy as jnp
from jax import lax
from jax.experimental import pallas as pl
from jax.experimental.pallas import tpu as pltpu
from jax.sharding import PartitionSpec as P

HEAD = 64
BUCKET = 4
REACH = 2
SIDE = 2 * REACH + 1
FAR = -128.0
LOW = -1e30
MESH = pl.DeviceIdType.MESH


def extended(cells, sides, width):
    for axis, dim in sides:
        count = lax.axis_size(axis)
        head = lax.slice_in_dim(cells, 0, width, axis=dim)
        tail = lax.slice_in_dim(cells, cells.shape[dim] - width, cells.shape[dim], axis=dim)
        cells = jnp.concatenate(
            [
                lax.ppermute(tail, axis, [(i, (i + 1) % count) for i in range(count)]),
                cells,
                lax.ppermute(head, axis, [((i + 1) % count, i) for i in range(count)]),
            ],
            axis=dim,
        )
    return cells


def banded(
    observations,
    send_counts,
    bucket_slots,
    latent,
    norm_gain,
    w_query,
    w_key,
    w_value,
    null_kv,
    rel_bias,
    w_out,
    w_up,
    w_down,
):
    counts = send_counts[0]
    places = bucket_slots.shape[2]
    half_chan = observations.shape[1]
    offsets = jnp.cumsum(counts) - counts
    within = jnp.arange(places, dtype=jnp.int32)
    active = within[None, :] < counts[:, None]
    picked = jnp.where(active, offsets[:, None] + within[None, :], 0)
    packed = jnp.where(active[:, :, None], observations[picked], jnp.zeros((), jnp.bfloat16))
    arrived = lax.all_to_all(packed, ("lat", "lon"), split_axis=0, concat_axis=0, tiled=True)
    lat_cells = latent.shape[0]
    lon_cells = latent.shape[1]
    slot_total = lat_cells * lon_cells * BUCKET
    target = bucket_slots[0].reshape(-1)
    slot_rows = (
        jnp.zeros((slot_total + 1, half_chan), jnp.bfloat16)
        .at[target]
        .set(arrived.reshape(-1, half_chan))
    )
    buckets = slot_rows[:slot_total].reshape(lat_cells, lon_cells, BUCKET, half_chan)
    rows_ext = lax.axis_index("lat") * lat_cells + jnp.arange(
        -REACH, lat_cells + REACH, dtype=jnp.int32
    )
    inside = (rows_ext >= 0) & (rows_ext < lat_cells * lax.axis_size("lat"))
    padded = extended(buckets, (("lat", 0), ("lon", 1)), REACH)
    padded = jnp.where(inside[:, None, None, None], padded, jnp.zeros((), jnp.bfloat16))
    widened = lax.all_gather(padded, "rep", axis=3, tiled=True)
    keys_ext = jnp.dot(widened, w_key, preferred_element_type=jnp.float32).astype(jnp.bfloat16)
    values_ext = jnp.dot(widened, w_value, preferred_element_type=jnp.float32).astype(jnp.bfloat16)
    filled_ext = jnp.any(widened != 0, axis=-1)
    lat_float = latent.astype(jnp.float32)
    inv_rms = lax.rsqrt(jnp.mean(lat_float * lat_float, axis=-1, keepdims=True) + 1e-06)
    normed = (lat_float * inv_rms * norm_gain).astype(jnp.bfloat16)
    queries = jnp.dot(normed, w_query, preferred_element_type=jnp.float32).astype(jnp.bfloat16)
    heads_here = w_query.shape[1] // HEAD
    window_side = 2 * REACH + 1
    wide_cols = lon_cells + 2 * REACH
    query_heads = queries.reshape(lat_cells, lon_cells, heads_here, HEAD)
    key_heads = keys_ext.reshape(lat_cells + 2 * REACH, wide_cols, BUCKET, heads_here, HEAD)
    value_heads = values_ext.reshape(lat_cells + 2 * REACH, wide_cols, BUCKET, heads_here, HEAD)
    null_key = null_kv[0].reshape(heads_here, HEAD)
    null_value = null_kv[1].astype(jnp.float32).reshape(heads_here, HEAD)
    score_scale = 1.0 / math.sqrt(HEAD)
    null_scores = (
        jnp.einsum("yxhe,he->hyx", query_heads, null_key, preferred_element_type=jnp.float32)
        * score_scale
    )
    score_parts = [null_scores[..., None]]
    for row_step in range(window_side):
        for col_step in range(window_side):
            place = row_step * window_side + col_step
            window_keys = key_heads[
                row_step : row_step + lat_cells, col_step : col_step + lon_cells
            ]
            local_scores = (
                jnp.einsum(
                    "yxhe,yxbhe->hyxb", query_heads, window_keys, preferred_element_type=jnp.float32
                )
                * score_scale
            )
            local_scores = local_scores + rel_bias[:, place][:, None, None, None]
            window_mask = filled_ext[
                row_step : row_step + lat_cells, col_step : col_step + lon_cells
            ]
            score_parts.append(jnp.where(window_mask[None], local_scores, -jnp.inf))
    scores = jnp.concatenate(score_parts, axis=-1)
    row_max = jnp.max(scores, axis=-1, keepdims=True)
    exponent = jnp.exp(scores - row_max)
    weights = (exponent / jnp.sum(exponent, axis=-1, keepdims=True)).astype(jnp.bfloat16)
    null_share = jnp.transpose(weights[..., 0], (1, 2, 0)).astype(jnp.float32)
    mixture = null_share[..., None] * null_value[None, None]
    for row_step in range(window_side):
        for col_step in range(window_side):
            place = row_step * window_side + col_step
            window_values = value_heads[
                row_step : row_step + lat_cells, col_step : col_step + lon_cells
            ]
            share = weights[..., 1 + place * BUCKET : 1 + (place + 1) * BUCKET]
            mixture = mixture + jnp.einsum(
                "hyxb,yxbhe->yxhe", share, window_values, preferred_element_type=jnp.float32
            )
    mixed = mixture.astype(jnp.bfloat16).reshape(lat_cells * lon_cells, heads_here * HEAD)
    attended = jnp.dot(mixed, w_out, preferred_element_type=jnp.float32)
    flat_normed = normed.reshape(lat_cells * lon_cells, -1)
    raised = lax.dot_general(
        flat_normed,
        lax.all_gather(w_up, "lat", axis=0, tiled=True),
        (((1,), (1,)), ((), ())),
        preferred_element_type=jnp.float32,
    )
    hidden = jax.nn.gelu(raised, approximate=True).astype(jnp.bfloat16)
    down_rows = lax.all_gather(w_down, "lat", axis=0, tiled=True)
    expanded = jnp.dot(hidden, down_rows, preferred_element_type=jnp.float32)
    combined = (attended + expanded).reshape(lat_cells, lon_cells, -1)
    summed = lax.psum_scatter(combined, "rep", scatter_dimension=0, tiled=True)
    share_rows = summed.shape[0]
    own_rows = lax.dynamic_slice_in_dim(
        lat_float, lax.axis_index("rep") * share_rows, share_rows, 0
    )
    return (own_rows + summed).astype(jnp.bfloat16)


def dot_nt(a, b):
    return lax.dot_general(a, b, (((1,), (1,)), ((), ())), preferred_element_type=jnp.float32)


def dot_nn(a, b):
    return jnp.dot(a, b, preferred_element_type=jnp.float32)


def fused_kernel(
    sizes,
    obs_hbm,
    counts_hbm,
    slots_hbm,
    lat_hbm,
    gain_hbm,
    wq_hbm,
    wk_hbm,
    wv_hbm,
    null_ref,
    bias_hbm,
    wo_hbm,
    up_hbm,
    down_hbm,
    out_ref,
    obs_ref,
    counts_ref,
    slots_ref,
    lat_ref,
    gain_ref,
    wq_ref,
    wk_ref,
    wv_ref,
    bias_ref,
    wo_ref,
    up_ref,
    down_ref,
    wq2_ref,
    wk2_ref,
    wv2_ref,
    head_ref,
    head2_ref,
    wo2_ref,
    up2_ref,
    down2_ref,
    tok_ref,
    back_ref,
    send_ref,
    part_ref,
    rows_ref,
    metas_ref,
    q_ref,
    k_ref,
    v_ref,
    near_ref,
    att_ref,
    load_sem,
    pair_send,
    pair_recv,
    tok_send,
    tok_recv,
    part_send,
    part_recv,
    obs_send,
    obs_recv,
    meta_send,
    meta_recv,
):
    n_lat, n_lon, lat_cells, lon_cells, heads = sizes
    half_rows = lat_cells // 2
    tokens = half_rows * lon_cells
    owners = n_lat * n_lon
    group = owners * 2
    cap = slots_ref.shape[2]
    listed = owners * cap
    total = owners * listed
    hops = n_lat - 1
    lat = lax.axis_index("lat")
    lon = lax.axis_index("lon")
    rep = lax.axis_index("rep")
    owner = lat * n_lon + lon
    me = owner * 2 + rep

    def member(flat):
        return {"lat": flat // (2 * n_lon), "lon": (flat // 2) % n_lon, "rep": flat % 2}

    barrier = pltpu.get_barrier_semaphore()
    for step in range(1, group):
        pl.semaphore_signal(
            barrier, inc=1, device_id=member((me + step) % group), device_id_type=MESH
        )

    half = pl.ds(rep * half_rows, half_rows)
    loads = [
        pltpu.make_async_copy(source, target, load_sem.at[index])
        for index, (source, target) in enumerate(
            (
                (lat_hbm.at[half], lat_ref),
                (gain_hbm, gain_ref),
                (obs_hbm, obs_ref),
                (counts_hbm, counts_ref),
                (slots_hbm, slots_ref),
                (bias_hbm, bias_ref),
                (up_hbm, up_ref),
                (down_hbm, down_ref),
                (wq_hbm, wq_ref),
                (wk_hbm, wk_ref),
                (wv_hbm, wv_ref),
                (wo_hbm, wo_ref),
            )
        )
    ]
    for load in loads:
        load.start()
    for load in loads[:6]:
        load.wait()

    x = lat_ref[...].astype(jnp.float32).reshape(tokens, lat_ref.shape[2])
    inv = lax.rsqrt(jnp.mean(x * x, axis=-1, keepdims=True) + 1e-06)
    normed = (x * inv * gain_ref[...]).astype(jnp.bfloat16)
    tok_ref[lat] = normed
    att_ref[...] = x

    entry = lax.broadcasted_iota(jnp.int32, (listed, owners), 0)
    column = lax.broadcasted_iota(jnp.int32, (listed, owners), 1)
    counts = counts_ref[...]
    first = jnp.sum(jnp.where(column < entry // cap, counts, 0), axis=1, keepdims=True)
    held = jnp.sum(jnp.where(column == entry // cap, counts, 0), axis=1, keepdims=True)
    place = entry[:, 0:1] % cap
    spots = lax.broadcasted_iota(jnp.int32, (listed, obs_ref.shape[0]), 1)
    pick = jnp.where((spots == first + place) & (place < held), 1.0, 0.0).astype(jnp.bfloat16)
    my_rows = pl.ds(pl.multiple_of(owner * listed, listed), listed)
    rows_ref[rep, my_rows, :] = dot_nn(pick, obs_ref[...]).astype(jnp.bfloat16)

    slots = slots_ref[0]
    row_slots = lon_cells * BUCKET
    cell_y = (lat * lat_cells + slots // row_slots).astype(jnp.float32)
    cell_x = (lon * lon_cells + (slots // BUCKET) % lon_cells).astype(jnp.float32)
    metas_ref[owner] = jnp.zeros(metas_ref.shape[1:], jnp.float32)
    metas_ref[owner, 0, :, 0:cap] = jnp.where(slots < lat_cells * row_slots, cell_y, FAR)
    metas_ref[owner, 1, :, 0:cap] = cell_x

    nulls = null_ref[...].astype(jnp.float32)
    head_ref[...] = jnp.zeros(head_ref.shape, jnp.float32)
    for h in range(heads):
        head_ref[h, 0:2, 0:HEAD] = nulls[:, h * HEAD : (h + 1) * HEAD]
        head_ref[h, 2:3, 0 : SIDE * SIDE] = bias_ref[h : h + 1, :]

    pl.semaphore_wait(barrier, group - 1)

    def pair_copy(index, source, target):
        return pltpu.make_async_remote_copy(
            src_ref=source,
            dst_ref=target,
            send_sem=pair_send.at[index],
            recv_sem=pair_recv.at[index],
            device_id={"rep": 1 - rep},
            device_id_type=MESH,
        )

    up_copy = pair_copy(0, up_hbm, up2_ref)
    down_copy = pair_copy(1, down_hbm, down2_ref)
    wq_copy = pair_copy(2, wq_hbm, wq2_ref)
    wk_copy = pair_copy(3, wk_hbm, wk2_ref)
    wv_copy = pair_copy(4, wv_hbm, wv2_ref)
    wo_copy = pair_copy(5, wo_hbm, wo2_ref)
    head_copy = pair_copy(6, head_ref, head2_ref)

    def within(index):
        return (index >= 0) & (index < n_lat)

    def tok_copy(way, hop, source):
        at = (way > 0) * hops + hop
        return pltpu.make_async_remote_copy(
            src_ref=tok_ref.at[source],
            dst_ref=tok_ref.at[source],
            send_sem=tok_send.at[at],
            recv_sem=tok_recv.at[at],
            device_id={"lat": lat + way},
            device_id_type=MESH,
        )

    def sum_copy(way, hop):
        at = (way > 0) * hops + hop
        return pltpu.make_async_remote_copy(
            src_ref=send_ref.at[at],
            dst_ref=part_ref.at[at],
            send_sem=part_send.at[at],
            recv_sem=part_recv.at[at],
            device_id={"lat": lat - way},
            device_id_type=MESH,
        )

    def obs_copy(step, who):
        other = (owner + step) % owners
        source_rows = pl.ds(pl.multiple_of(who * listed, listed), listed)
        return pltpu.make_async_remote_copy(
            src_ref=rows_ref.at[rep, source_rows],
            dst_ref=rows_ref.at[rep, source_rows],
            send_sem=obs_send.at[step],
            recv_sem=obs_recv.at[step],
            device_id={"lat": other // n_lon, "lon": other % n_lon},
            device_id_type=MESH,
        )

    def meta_copy(step, who):
        other = (owner + step) % owners
        return pltpu.make_async_remote_copy(
            src_ref=metas_ref.at[who],
            dst_ref=metas_ref.at[who],
            send_sem=meta_send.at[step],
            recv_sem=meta_recv.at[step],
            device_id={"lat": other // n_lon, "lon": other % n_lon},
            device_id_type=MESH,
        )

    ways = (1, -1)
    for way in ways:

        @pl.when(within(lat + way))
        def _():
            tok_copy(way, 0, lat).start()

    pair_copies = (up_copy, down_copy, wq_copy, wk_copy, wv_copy, wo_copy, head_copy)
    for copy in pair_copies:
        copy.start()
    for step in range(1, owners):
        obs_copy(step, owner).start()
        meta_copy(step, owner).start()
    rows_copy = pair_copy(7, rows_ref.at[rep], rows_ref.at[rep])
    back_rows = pair_copy(7, rows_ref.at[1 - rep], rows_ref.at[1 - rep])

    halves = ((up_ref, down_ref), (up2_ref, down2_ref))

    def fed(value):
        result = None
        for up, down in halves:
            hidden = jax.nn.gelu(dot_nt(value, up[...]), approximate=True).astype(jnp.bfloat16)
            term = dot_nn(hidden, down[...])
            result = term if result is None else result + term
        return result

    up_copy.wait_recv()
    down_copy.wait_recv()
    for load in loads[6:]:
        load.wait()

    for step in range(1, owners):
        obs_copy(step, (owner + owners - step) % owners).wait_recv()
    rows_copy.start()
    for step in range(1, owners):
        meta_copy(step, (owner + owners - step) % owners).wait_recv()

    lane = lax.broadcasted_iota(jnp.int32, (128, total), 1)
    line = lax.broadcasted_iota(jnp.int32, (128, total), 0)
    spread = jnp.where(lane % cap == line, 1.0, 0.0).astype(jnp.bfloat16)
    pair_lane = lax.broadcasted_iota(jnp.int32, (listed, total), 1)
    pair_line = lax.broadcasted_iota(jnp.int32, (listed, total), 0)
    wanted = (pair_lane // cap) % owners * owners + pair_lane // listed == pair_line

    def along(field):
        flat = metas_ref[:, field].reshape(listed, metas_ref.shape[3]).astype(jnp.bfloat16)
        chosen = jnp.where(wanted, dot_nn(flat, spread), 0.0)
        return jnp.sum(chosen, axis=0, keepdims=True)

    key_y = along(0)
    key_x = along(1)
    query_x = (
        lax.broadcasted_iota(jnp.int32, (lon_cells, total), 0) + lon * lon_cells
    ).astype(jnp.float32)
    wide = float(n_lon * lon_cells)
    off_x = key_x - query_x + float(REACH)
    off_x = jnp.where(off_x < 0, off_x + wide, off_x)
    near_ref[...] = jnp.where(off_x >= wide, off_x - wide, off_x)
    query_y = (
        lax.broadcasted_iota(jnp.int32, (half_rows, total), 0)
        + (lat * lat_cells + rep * half_rows)
    ).astype(jnp.float32)
    off_y = key_y - query_y + float(REACH)

    scale = 1.0 / math.sqrt(HEAD)

    def attend(wq, wk, wv, wo, per_head):
        widened = jnp.concatenate([rows_ref[0], rows_ref[1]], axis=1)
        queries = (dot_nn(normed, wq[...]).astype(jnp.bfloat16) * scale).astype(jnp.bfloat16)
        keys = dot_nn(widened, wk[...]).astype(jnp.bfloat16)
        values = dot_nn(widened, wv[...]).astype(jnp.bfloat16)
        for h in range(heads):
            lanes = slice(h * HEAD, (h + 1) * HEAD)
            q_ref[h] = queries[:, lanes]
            k_ref[h] = keys[:, lanes]
            v_ref[h] = values[:, lanes]

        def one_head(h, carry):
            q = q_ref[h]
            info = per_head[h]
            null_key = info[0:1, :HEAD]
            null_value = info[1:2, :HEAD]
            scores = dot_nt(q, k_ref[h])
            null_score = jnp.sum(q.astype(jnp.float32) * null_key, axis=1, keepdims=True)
            shifts = []
            for q_step in range(SIDE):
                shift = jnp.full(off_y.shape, LOW, jnp.float32)
                for p_step in range(SIDE):
                    at = p_step * SIDE + q_step
                    shift = jnp.where(off_y == float(p_step), info[2:3, at : at + 1], shift)
                shifts.append(shift)
            near = near_ref[...]
            biases = []
            for row in range(half_rows):
                bias = jnp.full(near.shape, LOW, jnp.float32)
                for q_step in range(SIDE):
                    bias = jnp.where(
                        near == float(q_step), shifts[q_step][row : row + 1, :], bias
                    )
                biases.append(bias)
            scores = scores + jnp.concatenate(biases, axis=0)
            top = jnp.maximum(jnp.max(scores, axis=1, keepdims=True), null_score)
            grown = jnp.exp(scores - top)
            null_grown = jnp.exp(null_score - top)
            share = 1.0 / (jnp.sum(grown, axis=1, keepdims=True) + null_grown)
            weights = (grown * share).astype(jnp.bfloat16)
            null_weight = (null_grown * share).astype(jnp.bfloat16).astype(jnp.float32)
            mixed = (dot_nn(weights, v_ref[h]) + null_weight * null_value).astype(jnp.bfloat16)
            rows = pl.ds(pl.multiple_of(h * HEAD, HEAD), HEAD)
            att_ref[...] += dot_nn(mixed, wo[rows, :])
            return carry

        lax.fori_loop(0, heads, one_head, 0)

    for hop in range(hops):
        if hop == hops - 1:
            back_rows.wait_recv()
            attend(wq_ref, wk_ref, wv_ref, wo_ref, head_ref)
        for way in ways:
            source = lat - way * (1 + hop)

            @pl.when(within(source))
            def _():
                tok_copy(way, hop, source).wait_recv()

            @pl.when(within(source) & within(lat + way))
            def _():
                tok_copy(way, hop + 1, source).start()

        for way in ways:
            source = lat - way * (1 + hop)
            at = (way > 0) * hops + hop

            @pl.when(within(source))
            def _():
                back_ref[at] = fed(tok_ref[source])

            @pl.when(within(source) & jnp.logical_not(within(lat + way)))
            def _():
                send_ref[at] = back_ref[at].astype(jnp.bfloat16)
                sum_copy(way, hop).start()

    for hop in range(hops - 2, -1, -1):
        for way in ways:
            source = lat - way * (1 + hop)
            at = (way > 0) * hops + hop

            @pl.when(within(source) & within(lat + way))
            def _():
                sum_copy(way, hop + 1).wait_recv()
                total_here = back_ref[at] + part_ref[at + 1].astype(jnp.float32)
                send_ref[at] = total_here.astype(jnp.bfloat16)
                sum_copy(way, hop).start()

    wq_copy.wait_recv()
    wk_copy.wait_recv()
    wv_copy.wait_recv()
    wo_copy.wait_recv()
    head_copy.wait_recv()
    att_ref[...] += fed(normed)
    attend(wq2_ref, wk2_ref, wv2_ref, wo2_ref, head2_ref)

    for way in ways:

        @pl.when(within(lat + way))
        def _():
            sum_copy(way, 0).wait_recv()
            att_ref[...] += part_ref[(way > 0) * hops].astype(jnp.float32)

    out_ref[...] = att_ref[...].astype(jnp.bfloat16)

    for way in ways:
        for hop in range(hops):

            @pl.when(within(lat - way * hop) & within(lat + way))
            def _():
                tok_copy(way, hop, lat - way * hop).wait_send()

            @pl.when(within(lat - way * (1 + hop)))
            def _():
                sum_copy(way, hop).wait_send()

    for copy in pair_copies:
        copy.wait_send()
    rows_copy.wait_send()
    for step in range(1, owners):
        obs_copy(step, owner).wait_send()
        meta_copy(step, owner).wait_send()


def fused(
    n_lat,
    n_lon,
    observations,
    send_counts,
    bucket_slots,
    latent,
    norm_gain,
    w_query,
    w_key,
    w_value,
    null_kv,
    rel_bias,
    w_out,
    w_up,
    w_down,
):
    lat_cells, lon_cells, depth = latent.shape
    owners = n_lat * n_lon
    cap = bucket_slots.shape[2]
    total = owners * owners * cap
    half_chan = observations.shape[1]
    heads = w_query.shape[1] // HEAD
    tokens = lat_cells * lon_cells // 2
    lanes = 128
    hops = n_lat - 1
    bf16 = jnp.bfloat16
    args = (
        observations,
        send_counts,
        bucket_slots,
        latent,
        norm_gain,
        w_query,
        w_key,
        w_value,
        null_kv,
        rel_bias,
        w_out,
        w_up,
        w_down,
    )
    specs = [pl.BlockSpec(memory_space=pltpu.HBM)] * len(args)
    specs[8] = pl.BlockSpec(memory_space=pltpu.VMEM)
    head_shape = (heads, 8, lanes)
    dma = pltpu.SemaphoreType.DMA
    out = pl.pallas_call(
        functools.partial(fused_kernel, (n_lat, n_lon, lat_cells, lon_cells, heads)),
        out_shape=jax.ShapeDtypeStruct((tokens, depth), bf16),
        in_specs=specs,
        out_specs=pl.BlockSpec(memory_space=pltpu.VMEM),
        scratch_shapes=[
            pltpu.VMEM(observations.shape, bf16),
            pltpu.VMEM(send_counts.shape, jnp.int32),
            pltpu.VMEM(bucket_slots.shape, jnp.int32),
            pltpu.VMEM((lat_cells // 2, lon_cells, depth), bf16),
            pltpu.VMEM(norm_gain.shape, jnp.float32),
            pltpu.VMEM(w_query.shape, bf16),
            pltpu.VMEM(w_key.shape, bf16),
            pltpu.VMEM(w_value.shape, bf16),
            pltpu.VMEM(rel_bias.shape, jnp.float32),
            pltpu.VMEM(w_out.shape, bf16),
            pltpu.VMEM(w_up.shape, bf16),
            pltpu.VMEM(w_down.shape, bf16),
            pltpu.VMEM(w_query.shape, bf16),
            pltpu.VMEM(w_key.shape, bf16),
            pltpu.VMEM(w_value.shape, bf16),
            pltpu.VMEM(head_shape, jnp.float32),
            pltpu.VMEM(head_shape, jnp.float32),
            pltpu.VMEM(w_out.shape, bf16),
            pltpu.VMEM(w_up.shape, bf16),
            pltpu.VMEM(w_down.shape, bf16),
            pltpu.VMEM((n_lat, tokens, depth), bf16),
            pltpu.VMEM((2 * hops, tokens, depth), jnp.float32),
            pltpu.VMEM((2 * hops, tokens, depth), bf16),
            pltpu.VMEM((2 * hops, tokens, depth), bf16),
            pltpu.VMEM((2, total, half_chan), bf16),
            pltpu.VMEM((owners, 2, owners, lanes), jnp.float32),
            pltpu.VMEM((heads, tokens, HEAD), bf16),
            pltpu.VMEM((heads, total, HEAD), bf16),
            pltpu.VMEM((heads, total, HEAD), bf16),
            pltpu.VMEM((lon_cells, total), jnp.float32),
            pltpu.VMEM((tokens, depth), jnp.float32),
            dma((12,)),
            dma((8,)),
            dma((8,)),
            dma((2 * hops,)),
            dma((2 * hops,)),
            dma((2 * hops,)),
            dma((2 * hops,)),
            dma((owners,)),
            dma((owners,)),
            dma((owners,)),
            dma((owners,)),
        ],
        compiler_params=pltpu.CompilerParams(
            collective_id=0, has_side_effects=True, vmem_limit_bytes=48 * 2**20
        ),
    )(*args)
    return out.reshape(lat_cells // 2, lon_cells, depth)


def solution(mesh):
    in_specs = (
        P(("parts", "lat", "lon"), "rep"),
        P(("parts", "lat", "lon"), None),
        P(("parts", "lat", "lon"), None, None),
        P(("parts", "lat"), "lon", None),
        P(),
        P(None, "rep"),
        P(None, "rep"),
        P(None, "rep"),
        P(None, "rep"),
        P("rep", None),
        P("rep", None),
        P(("lat", "rep"), None),
        P(("lat", "rep"), None),
    )
    out_specs = P(("parts", "lat", "rep"), "lon", None)
    n_lat, n_lon, n_rep = mesh.shape["lat"], mesh.shape["lon"], mesh.shape["rep"]

    def local(observations, send_counts, bucket_slots, *rest):
        cap = bucket_slots.shape[2]
        listed = n_lat * n_lon * cap
        direct = (
            n_rep == 2
            and n_lat in (2, 4)
            and listed <= 128
            and cap == n_lat * n_lon
        )
        step = functools.partial(fused, n_lat, n_lon) if direct else banded
        return step(observations, send_counts, bucket_slots, *rest)

    return jax.shard_map(local, mesh=mesh, in_specs=in_specs, out_specs=out_specs, check_vma=False)
```
